32 devices in a mesh: row: 4 (over z), col: 8 (over y, x, core).
Axes of the slice: x: 2, y: 2, z: 4, core: 2. Of those that a mesh axis runs over, the one named last changes fastest.
Arguments:
- multipliers: bfloat16 [128, 32768], P('col', 'row'), may hold values from -6 to 6
- source: float32 [128, 32768], P('col', 'row'), may hold values from -6 to 6
- denominator: float32 [128, 32768], P('col', 'row'), may hold values from 0.8 to 6
- cycle: bfloat16 [32768, 32768], P('col', 'row'), may hold values from -0.03125 to 0.03125
Outputs:
- updated: bfloat16 [128, 32768], P('col', 'row')
The draws below stay inside these ranges and needn't reach their ends.
All inputs are finite; a program needn't handle non-finite values.
Results may differ from the reference program's by a relative error of at most 0.015.
Values may be sent and summed in bfloat16 or wider, within the bound.
No kernel may reach another device: no remote copies, remote signals or barrier semaphores. Data moves between devices by JAX's collectives and lax.ppermute only.
A program may use at most 128 MiB of HBM per device.

```python
import math
import jax
import jax.numpy as jnp
from jax import lax

ITERS = 2
K = 32768
ROWS = 128


def block_scale(own_key, dims, split, low, high):
    def one(dim, parts):
        steps = jax.random.uniform(jax.random.fold_in(jax.random.fold_in(own_key, 6), dim), (parts,), jnp.float32, low / len(split), high / len(split))
        return jnp.repeat(jnp.exp(steps), dims[dim] // parts).reshape((-1,) + (1,) * (len(dims) - dim - 1))

    loudness = one(*split[0])
    for cut in split[1:]:
        loudness = loudness * one(*cut)
    return loudness


def centred(rng, extent, width, most, pieces=(), held_as=jnp.bfloat16):
    array = jax.random.normal(rng, extent, jnp.float32) * width
    if len(pieces) > 0:
        array = block_scale(rng, extent, pieces, -0.22, 0.18) * array
    return jnp.clip(array, min=-most, max=most).astype(held_as)


def setup_inputs(seed: int = 0) -> dict:
    keys = jax.random.split(jax.random.key(seed), 5)
    multipliers = centred(keys[0], (ROWS, K), 1.0, 6.0, ((0, 8), (1, 4)))
    source = centred(keys[1], (ROWS, K), 1.0, 6.0, ((0, 8), (1, 4)), jnp.float32)
    denominator = jnp.clip(jnp.exp(math.log(6.0) - 2.014903 * jax.random.uniform(keys[2], (ROWS, K), jnp.float32) ** block_scale(keys[2], (ROWS, K), ((0, 8), (1, 4)), -0.2, 0.2)), 0.8, 6.0)
    cycle = centred(keys[3], (K, K), K ** -0.5, 0.03125, ((0, 8), (1, 4)))
    return dict(multipliers=multipliers, source=source, denominator=denominator, cycle=cycle)


def reference(multipliers, source, denominator, cycle):
    current = multipliers
    blocks = 16
    block_width = K // blocks
    for sweep in range(ITERS):
        def column_block(index):
            piece_cols = lax.dynamic_slice_in_dim(cycle, index * block_width, block_width, 1)
            return jnp.dot(current, piece_cols, preferred_element_type=jnp.float32)

        stacked = lax.map(column_block, jnp.arange(blocks, dtype=jnp.int32))
        product = jnp.transpose(stacked, (1, 0, 2)).reshape(ROWS, K)
        current = ((source + product) / denominator).astype(jnp.bfloat16)
    return current
```

```python
import jax
import jax.numpy as jnp
from jax import lax
from jax.experimental import pallas as pl
from jax.experimental.pallas import tpu as pltpu
from jax.sharding import PartitionSpec as P

ITERS = 2
CORES = 2
HELD_BYTES = 32 << 20
LIMIT_BYTES = 8 << 20
TILE = 512
PIECE_ROWS = 512

VMEM = pl.BlockSpec(memory_space=pltpu.VMEM)
HBM = pl.BlockSpec(memory_space=pl.ANY)


def hold(cycle, start):
    rows, cols = cycle.shape[0] - start, cycle.shape[1]
    count = rows // PIECE_ROWS

    def kernel(cycle_ref, *refs):
        copies = [
            pltpu.make_async_copy(
                cycle_ref.at[pl.ds(start + index * PIECE_ROWS, PIECE_ROWS)], refs[index], refs[count].at[index]
            )
            for index in range(count)
        ]
        for copy in copies:
            copy.start()
        for copy in copies:
            copy.wait()

    return pl.pallas_call(
        kernel,
        in_specs=[HBM],
        out_specs=[VMEM] * count,
        out_shape=[pltpu.VMEM((PIECE_ROWS, cols), cycle.dtype)] * count,
        scratch_shapes=[pltpu.SemaphoreType.DMA((count,))],
        compiler_params=pltpu.CompilerParams(vmem_limit_bytes=1 << 20),
        cost_estimate=pl.CostEstimate(flops=0, bytes_accessed=2 * rows * cols * 2, transcendentals=0),
        name="hold",
    )(cycle)


def project(blocks, held, cycle, base_of, width, finish, outs, name):
    count = len(blocks)
    block_rows, depth = blocks[0].shape
    pieces = len(held)
    streamed = depth - pieces * PIECE_ROWS
    tile = min(TILE, width)
    steps = width // tile

    def kernel(*refs):
        block_refs = refs[:count]
        held_refs, cycle_ref = refs[count : count + pieces], refs[count + pieces]
        out_refs = refs[count + pieces + 1 : count + pieces + 1 + len(outs)]
        lhs, buffer, sems = refs[count + pieces + 1 + len(outs) :]
        base = base_of()

        def columns(step):
            return pl.ds(pl.multiple_of(base + step * tile, tile), tile)

        def fetch(step):
            return pltpu.make_async_copy(
                cycle_ref.at[pl.ds(0, streamed), columns(step)], buffer.at[lax.rem(step, 2)], sems.at[lax.rem(step, 2)]
            )

        if streamed:
            for step in range(min(2, steps)):
                fetch(jnp.int32(step)).start()
        for index in range(count):
            lhs[index * block_rows : (index + 1) * block_rows, :] = block_refs[index][...]
        def body(step, carry):
            total = 0.0
            for index, held_ref in enumerate(held_refs):
                at = streamed + index * PIECE_ROWS
                total += jnp.dot(
                    lhs[:, at : at + PIECE_ROWS], held_ref[:, columns(step)], preferred_element_type=jnp.float32
                )
            if streamed:
                fetch(step).wait()
                total += jnp.dot(lhs[:, :streamed], buffer[lax.rem(step, 2)], preferred_element_type=jnp.float32)

                @pl.when(step + 2 < steps)
                def _():
                    fetch(step + 2).start()

            finish(total, pl.ds(pl.multiple_of(step * tile, tile), tile), out_refs)
            return carry

        lax.fori_loop(0, steps, body, 0)

    rows = count * block_rows
    return pl.pallas_call(
        kernel,
        in_specs=[VMEM] * (count + pieces) + [HBM],
        out_specs=[VMEM] * len(outs),
        out_shape=outs,
        scratch_shapes=[
            pltpu.VMEM((rows, depth), jnp.bfloat16),
            pltpu.VMEM((2, max(streamed, 16), tile), jnp.bfloat16),
            pltpu.SemaphoreType.DMA((2,)),
        ],
        compiler_params=pltpu.CompilerParams(vmem_limit_bytes=LIMIT_BYTES),
        cost_estimate=pl.CostEstimate(
            flops=2 * rows * depth * width, bytes_accessed=2 * streamed * width, transcendentals=0
        ),
        name=name,
    )(*blocks, *held, cycle)


def add_split(keep, received, slot_of, count, name):
    rows, width = keep.shape
    block_rows = rows // count

    def kernel(keep_ref, received_ref, *out_refs):
        for k in range(count):
            at = pl.ds(pl.multiple_of(slot_of(k) * block_rows, block_rows), block_rows)
            total = keep_ref[at, :] + received_ref[at, :].astype(jnp.float32)
            out_refs[k][...] = total.astype(out_refs[k].dtype)

    outs = [jax.ShapeDtypeStruct((block_rows, width), jnp.float32)]
    outs += [jax.ShapeDtypeStruct((block_rows, width), jnp.bfloat16)] * (count - 1)
    return pl.pallas_call(
        kernel,
        in_specs=[VMEM] * 2,
        out_specs=[VMEM] * count,
        out_shape=outs,
        compiler_params=pltpu.CompilerParams(vmem_limit_bytes=LIMIT_BYTES),
        cost_estimate=pl.CostEstimate(flops=rows * width, bytes_accessed=8 * rows * width, transcendentals=0),
        name=name,
    )(keep, received)


def shards(multipliers, source, denominator, cycle):
    planes, lanes = lax.axis_size("row"), lax.axis_size("col")
    chips = lanes // CORES
    local_rows, local_cols = multipliers.shape
    half = local_cols // CORES
    depth = cycle.shape[0]
    block_rows = local_rows * CORES
    total_rows = local_rows * lanes

    def place():
        lane = lax.axis_index("col")
        return lax.axis_index("row"), lane // CORES, lax.rem(lane, CORES)

    plane, chip, core = place()
    first = core == 0
    core_swap = [(i, i ^ 1) for i in range(lanes)]
    chip_swap = [[(i, i ^ (k * CORES)) for i in range(lanes)] for k in range(chips)]
    turn = [
        [
            ((z * chips + p) * CORES + c, ((p ^ k) * chips + z) * CORES + c)
            for z in range(planes)
            for p in range(chips)
            for c in range(CORES)
        ]
        for k in range(planes)
    ]

    def pair(array):
        low, high = array[:, :half], array[:, half:]
        mine = jnp.where(first, low, high)
        theirs = lax.ppermute(jnp.where(first, high, low), "col", core_swap)
        return jnp.concatenate(
            [jnp.where(first, mine, theirs), jnp.where(first, theirs, mine)], axis=0
        )

    def slot_of(k):
        z, p, _ = place()
        return z ^ p ^ k

    def scatter_add(keep, received, name):
        own, *others = add_split(keep, received, slot_of, chips, name)
        parts = [own]
        for k in range(1, chips):
            parts.append(lax.ppermute(others[k - 1], "col", chip_swap[k]).astype(jnp.float32))
        return sum(parts[1:], parts[0])

    def realign(current):
        return [lax.ppermute(current, ("row", "col"), turn[k]) for k in range(planes)]

    per_row = local_cols * 2
    held_rows = min(depth, HELD_BYTES // per_row) // PIECE_ROWS * PIECE_ROWS
    held = hold(cycle, depth - held_rows)
    current = pair(multipliers)
    source_pair, denominator_pair = pair(source), pair(denominator)

    for sweep in range(ITERS):
        blocks = realign(current)
        if sweep < ITERS - 1:
            def store(total, at, out_refs):
                out_refs[0][:, at] = total.astype(out_refs[0].dtype)

            send, = project(
                blocks, held, cycle, lambda: (1 - place()[2]) * half, half, store,
                [jax.ShapeDtypeStruct((total_rows, half), jnp.bfloat16)], "project_send",
            )
            received = lax.ppermute(send, "col", core_swap)
            keep, = project(
                blocks, held, cycle, lambda: place()[2] * half, half, store,
                [jax.ShapeDtypeStruct((total_rows, half), jnp.float32)], "project_keep",
            )
            product = scatter_add(keep, received, "add_columns")
            current = ((source_pair + product) / denominator_pair).astype(jnp.bfloat16)
        else:
            def store(total, at, out_refs):
                mine = place()[2] == 0
                for index in range(chips):
                    row = index * block_rows
                    low, high = total[row : row + local_rows], total[row + local_rows : row + block_rows]
                    to = slice(index * local_rows, (index + 1) * local_rows)
                    out_refs[0][to, at] = jnp.where(mine, low, high)
                    out_refs[1][to, at] = jnp.where(mine, high, low).astype(jnp.bfloat16)

            keep, send = project(
                blocks, held, cycle, lambda: 0, local_cols, store,
                [
                    jax.ShapeDtypeStruct((total_rows // CORES, local_cols), jnp.float32),
                    jax.ShapeDtypeStruct((total_rows // CORES, local_cols), jnp.bfloat16),
                ], "project_rows",
            )
            received = lax.ppermute(send, "col", core_swap)
            product = scatter_add(keep, received, "add_rows")
            current = ((source + product) / denominator).astype(jnp.bfloat16)
    return current


def solution(mesh):
    placed = (P("col", "row"), P("col", "row"), P("col", "row"), P("col", "row"))
    return jax.shard_map(
        shards, mesh=mesh, in_specs=placed, out_specs=P("col", "row"), check_vma=False
    )
```

```python
import jax
import jax.numpy as jnp
from jax import lax
from jax.experimental import pallas as pl
from jax.experimental.pallas import tpu as pltpu
from jax.sharding import PartitionSpec as P

ITERS = 2
CORES = 2
CHUNKS = 2
TILE = 512
PIECE_ROWS = 256
SOON_ROWS = 1024
LIMIT_BYTES = 6144 << 10
STREAM_LIMIT_BYTES = 8192 << 10
HELD_BYTES = 36 << 20
BUFFERS = 3

VMEM = pl.BlockSpec(memory_space=pltpu.VMEM)
HBM = pl.BlockSpec(memory_space=pl.ANY)


def place():
    lane = lax.axis_index("col")
    return lax.axis_index("row"), lane // CORES, lax.rem(lane, CORES)


def call(kernel, args, in_specs, outs, scratch, name, flops, moved, limit=LIMIT_BYTES):
    return pl.pallas_call(
        kernel,
        in_specs=in_specs,
        out_specs=[VMEM] * len(outs),
        out_shape=outs,
        scratch_shapes=scratch,
        compiler_params=pltpu.CompilerParams(vmem_limit_bytes=limit),
        cost_estimate=pl.CostEstimate(flops=flops, bytes_accessed=moved, transcendentals=0),
        name=name,
    )(*args)


def shape(rows, cols, dtype=jnp.bfloat16):
    return jax.ShapeDtypeStruct((rows, cols), dtype)


def hold(cycle, start, rows, after):
    cols = cycle.shape[1]
    piece = min(PIECE_ROWS, rows)
    count = rows // piece

    def kernel(cycle_ref, after_ref, *refs):
        copies = [
            pltpu.make_async_copy(
                cycle_ref.at[pl.ds(start + index * piece, piece)], refs[index], refs[count + 1].at[index]
            )
            for index in range(count)
        ]
        for copy in copies:
            copy.start()
        for copy in copies:
            copy.wait()
        refs[count][...] = jnp.zeros_like(refs[count])

    return call(
        kernel, [cycle, after], [HBM, HBM],
        [pltpu.VMEM((piece, cols), cycle.dtype)] * count + [shape(8, 128, jnp.float32)],
        [pltpu.SemaphoreType.DMA((count,))], "hold", 0, 2 * rows * cols * 2, 1 << 20,
    )


def gather_rows(block_refs, lhs):
    rows = block_refs[0].shape[0]
    for index, ref in enumerate(block_refs):
        lhs[index * rows : (index + 1) * rows, :] = ref[...]


def stream_dot(blocks, cycle, held, columns, width, name):
    count, pieces, parts = len(blocks), len(held), len(columns)
    block_rows, depth = blocks[0].shape
    piece = held[0].shape[0] if held else 0
    streamed = depth - pieces * piece
    tile = min(TILE, width)
    steps = width // tile
    rows = count * block_rows

    def kernel(*refs):
        held_refs, cycle_ref = refs[count : count + pieces], refs[count + pieces]
        out_refs = refs[count + pieces + 1 : count + pieces + 1 + parts]
        lhs, buffer, sems = refs[count + pieces + 1 + parts :]

        def column_of(n, step):
            return pl.ds(pl.multiple_of(columns[n](step * tile), tile), tile)

        def fetch(n, step):
            slot = (n * steps + step) % BUFFERS
            return pltpu.make_async_copy(
                cycle_ref.at[pl.ds(0, streamed), column_of(n, step)], buffer.at[slot], sems.at[slot]
            )

        order = [(n, step) for n in range(parts) for step in range(steps)]
        for at in order[:BUFFERS]:
            fetch(*at).start()
        gather_rows(refs[:count], lhs)
        for index, (n, step) in enumerate(order):
            fetch(n, step).wait()
            total = jnp.dot(lhs[:, :streamed], buffer[index % BUFFERS], preferred_element_type=jnp.float32)
            if index + BUFFERS < len(order):
                fetch(*order[index + BUFFERS]).start()
            for k, held_ref in enumerate(held_refs):
                at = streamed + k * piece
                total += jnp.dot(
                    lhs[:, at : at + piece], held_ref[:, column_of(n, step)], preferred_element_type=jnp.float32
                )
            out_refs[n][:, step * tile : (step + 1) * tile] = total

    return call(
        kernel, [*blocks, *held, cycle], [VMEM] * (count + pieces) + [HBM],
        [pltpu.VMEM((rows, width), jnp.float32)] * parts,
        [
            pltpu.VMEM((rows, depth), jnp.bfloat16),
            pltpu.VMEM((BUFFERS, streamed, tile), jnp.bfloat16),
            pltpu.SemaphoreType.DMA((BUFFERS,)),
        ],
        name, 2 * rows * depth * width * parts, 2 * streamed * width * parts, STREAM_LIMIT_BYTES,
    )


def held_dot(blocks, held, partial, column_of, store, outs, name):
    count, pieces = len(blocks), len(held)
    block_rows, depth = blocks[0].shape
    rows, width = partial.shape
    piece = held[0].shape[0]
    tile = min(TILE, width)
    steps = width // tile

    def kernel(*refs):
        held_refs, partial_ref = refs[count : count + pieces], refs[count + pieces]
        out_refs, lhs = refs[count + pieces + 1 : -1], refs[-1]
        gather_rows(refs[:count], lhs)
        for step in range(steps):
            total = partial_ref[:, step * tile : (step + 1) * tile]
            for index, held_ref in enumerate(held_refs):
                total += jnp.dot(
                    lhs[:, index * piece : (index + 1) * piece],
                    held_ref[:, pl.ds(pl.multiple_of(column_of(step * tile), tile), tile)],
                    preferred_element_type=jnp.float32,
                )
            store(total, step * tile, tile, out_refs)

    return call(
        kernel, [*blocks, *held, partial], [VMEM] * (count + pieces + 1), outs,
        [pltpu.VMEM((rows, depth), jnp.bfloat16)], name, 2 * rows * depth * width, 0,
    )


def add_split(keep, received, count, name):
    rows, width = keep.shape
    block_rows = rows // count

    def kernel(keep_ref, received_ref, *out_refs):
        for k in range(count):
            at = slice(k * block_rows, (k + 1) * block_rows)
            total = keep_ref[at, :] + received_ref[at, :].astype(jnp.float32)
            out_refs[k][...] = total.astype(out_refs[k].dtype)

    outs = [shape(block_rows, width, jnp.float32)] + [shape(block_rows, width)] * (count - 1)
    return call(kernel, [keep, received], [VMEM] * 2, outs, [], name, rows * width, 8 * rows * width)


def pick(planes, after, name):
    count = len(planes)

    def kernel(*refs):
        z, p, _ = place()
        for k in range(count):
            for source in range(count):
                @pl.when((z ^ p ^ k) == source)
                def _():
                    refs[count + len(after) + k][...] = refs[source][...]

    size = planes[0].size
    return call(
        kernel, [*planes, *after], [VMEM] * count + [HBM] * len(after), [shape(*planes[0].shape)] * count, [], name, 0, 4 * count * size
    )


def shards(multipliers, source, denominator, cycle):
    planes, lanes = lax.axis_size("row"), lax.axis_size("col")
    chips = lanes // CORES
    local_rows, local_cols = multipliers.shape
    half = local_cols // CORES
    part = half // CHUNKS
    wide = local_cols // CHUNKS
    block_rows = local_rows * CORES
    total_rows = local_rows * lanes

    first = place()[2] == 0
    core_swap = [(i, i ^ 1) for i in range(lanes)]
    chip_swap = [[(i, i ^ (k * CORES)) for i in range(lanes)] for k in range(chips)]
    plane_swap = [[(i, i ^ k) for i in range(planes)] for k in range(planes)]

    def pair(array):
        low, high = array[:, :half], array[:, half:]
        mine = jnp.where(first, low, high)
        theirs = lax.ppermute(jnp.where(first, high, low), "col", core_swap)
        top, bottom = jnp.where(first, mine, theirs), jnp.where(first, theirs, mine)
        return [
            jnp.concatenate([top[:, n * part : (n + 1) * part], bottom[:, n * part : (n + 1) * part]], axis=0)
            for n in range(CHUNKS)
        ]

    far = planes // 2

    def set_out(chunk):
        return {0: chunk, far: lax.ppermute(chunk, "row", plane_swap[far]), 1: lax.ppermute(chunk, "row", plane_swap[1])}

    def go_on(seen):
        for k in range(1, planes):
            low = k & -k
            if k not in seen:
                seen[k] = lax.ppermute(seen[k ^ low], "row", plane_swap[low])

    def tie(*arrays):
        return lax.optimization_barrier(arrays)

    def deal(seen, after=()):
        picked = pick([seen[k] for k in range(planes)], after, "pick")
        return [picked[0]] + [lax.ppermute(picked[k], "col", chip_swap[k]) for k in range(1, chips)]

    def scatter_add(keep, received, name):
        own, *others = add_split(keep, received, chips, name)
        for k in range(1, chips):
            own = own + lax.ppermute(others[k - 1], "col", chip_swap[k]).astype(jnp.float32)
        return own

    def column_in_halves(n):
        def column_of(at):
            core = place()[2]
            away = at < part
            return jnp.where(away, (1 - core) * half + n * part + at, core * half + n * part + at - part)

        return column_of

    def column_in_order(n):
        return lambda at: n * wide + at

    def store_halves(total, at, tile, out_refs):
        if at < part:
            out_refs[0][:, at : at + tile] = total.astype(jnp.bfloat16)
        else:
            out_refs[1][:, at - part : at - part + tile] = total

    def store_rows(total, at, tile, out_refs):
        mine = place()[2] == 0
        for index in range(chips):
            row = index * block_rows
            low, high = total[row : row + local_rows], total[row + local_rows : row + block_rows]
            to = slice(index * local_rows, (index + 1) * local_rows)
            out_refs[0][to, at : at + tile] = jnp.where(mine, high, low).astype(jnp.bfloat16)
            out_refs[1][to, at : at + tile] = jnp.where(mine, low, high)

    current = pair(multipliers)
    budget = HELD_BYTES // (2 * local_cols)
    streamed = min(part, max(PIECE_ROWS, cycle.shape[0] - budget))
    early = (part - streamed) // PIECE_ROWS
    held_rows = cycle.shape[0] - streamed
    soon = min(SOON_ROWS, held_rows - PIECE_ROWS)

    for sweep in range(ITERS):
        last = sweep == ITERS - 1
        columns = column_in_order if last else column_in_halves
        here, later = current
        seen, done = set_out(here), []
        if sweep == 0:
            *held, token = hold(cycle, streamed, soon, here)
            done = [token]
        later, seen[far], seen[1], *done = tie(later, seen[far], seen[1], *done)
        seen_later = set_out(later)
        if sweep == 0:
            *more, token = hold(cycle, streamed + soon, held_rows - soon, seen[far])
            held += more
            seen_later[far], token = tie(seen_later[far], token)
            source, denominator, token = tie(source, denominator, token)
            source_pair, denominator_pair = pair(source), pair(denominator)
            done.append(token)
        go_on(seen)
        go_on(seen_later)
        blocks = [deal(seen), deal(seen_later, done)]
        partial = stream_dot(
            blocks[0], cycle, held[:early], [columns(n) for n in range(CHUNKS)], wide, "stream_dot"
        )
        current = []
        for n in range(CHUNKS):
            if last:
                rows, width, store = total_rows // CORES, wide, store_rows
                src, den = source[:, n * wide : (n + 1) * wide], denominator[:, n * wide : (n + 1) * wide]
            else:
                rows, width, store = total_rows, part, store_halves
                src, den = source_pair[n], denominator_pair[n]
            send, keep = held_dot(
                blocks[1], held[early:], partial[n], columns(n), store,
                [shape(rows, width), shape(rows, width, jnp.float32)], "held_dot",
            )
            received = lax.ppermute(send, "col", core_swap)
            product = scatter_add(keep, received, "add_split")
            current.append(((src + product) / den).astype(jnp.bfloat16))
    return jnp.concatenate(current, axis=1)


def solution(mesh):
    placed = (P("col", "row"), P("col", "row"), P("col", "row"), P("col", "row"))
    return jax.shard_map(
        shards, mesh=mesh, in_specs=placed, out_specs=P("col", "row"), check_vma=False
    )
```
